32 devices in a mesh: shots: 4 (over y, core), band: 8 (over z, x).
Axes of the slice: x: 2, y: 2, z: 4, core: 2. Of those that a mesh axis runs over, the one named last changes fastest.
Arguments:
- forward: bfloat16 [4, 18, 32, 32, 512], P('shots', None, None, 'band'), may hold values from -6 to 6
- adjoint: bfloat16 [4, 16, 32, 32, 512], P('shots', None, None, 'band'), may hold values from -6 to 6
- velocity: float32 [32, 32, 512], P(None, 'band'), may hold values from 1.5 to 4.5
- hessian: float32 [32, 32, 512], P('band'), may hold values from 0.1 to 2
Outputs:
- gradient: float32 [32, 32, 512], P('band', None, 'shots')
The draws below stay inside these ranges and needn't reach their ends.
All inputs are finite; a program needn't handle non-finite values.
Results may differ from the reference program's by a relative error of at most 0.0003.
Values sent between devices are 32-bit elements; how exact they have to be, the bound alone decides.
A program may use at most 128 MiB of HBM per device.

```python
import math
import jax
import jax.numpy as jnp

NY = 512
TS = 16
GROUPS = 4
NX = 32
NZ = 32


def steps_of(rng, dims, pieces, smallest, largest):
    loudness = 1.0
    for axis_at, blocks in pieces:
        draws = jax.random.uniform(jax.random.fold_in(jax.random.fold_in(rng, 6), axis_at), (blocks,), jnp.float32, smallest / len(pieces), largest / len(pieces))
        loudness = loudness * jnp.repeat(jnp.exp(draws), dims[axis_at] // blocks).reshape((-1,) + (1,) * (len(dims) - 1 - axis_at))
    return loudness


def centred(rng, extent, scale, reach, shards=(), dtype=jnp.bfloat16):
    result = jax.random.normal(rng, extent, jnp.float32) * scale
    if len(shards) > 0:
        result = steps_of(rng, extent, shards, -0.22, 0.18) * result
    return jnp.clip(result, min=-reach, max=reach).astype(dtype)


def setup_inputs(seed: int = 0) -> dict:
    seeds = jax.random.split(jax.random.key(seed), 5)
    forward = centred(seeds[0], (GROUPS, TS + 2, NZ, NX, NY), 1.0, 6.0, ((0, 4), (3, 8)))
    adjoint = centred(seeds[1], (GROUPS, TS, NZ, NX, NY), 1.0, 6.0, ((0, 4), (3, 8)))
    velocity = jnp.clip(jnp.exp(math.log(4.5) - 1.0986123 * jax.random.uniform(seeds[2], (NZ, NX, NY), jnp.float32) ** steps_of(seeds[2], (NZ, NX, NY), ((1, 8),), -0.2, 0.2)), 1.5, 4.5)
    hessian = jnp.clip(jnp.exp(math.log(2.0) - 2.9957323 * jax.random.uniform(seeds[3], (NZ, NX, NY), jnp.float32) ** steps_of(seeds[3], (NZ, NX, NY), ((0, 8),), -0.2, 0.2)), 0.1, 2.0)
    return dict(forward=forward, adjoint=adjoint, velocity=velocity, hessian=hessian)


def reference(forward, adjoint, velocity, hessian):
    total = jnp.zeros(velocity.shape, jnp.float32)
    scale = 2.0 / (TS * velocity ** 3)
    for group in range(GROUPS):
        stored = forward[group].astype(jnp.float32)
        acceleration = stored[2:] - 2.0 * stored[1:-1] + stored[:-2]
        correlation = jnp.sum(adjoint[group].astype(jnp.float32) * acceleration, axis=0)
        total = total + correlation * scale
    return total / (hessian + 0.05)
```

```python
import functools

import jax
import jax.numpy as jnp
from jax import lax
from jax.experimental import pallas as pl
from jax.experimental.pallas import tpu as pltpu
from jax.sharding import PartitionSpec as P

damping = 0.05
MESH = pl.DeviceIdType.MESH


def kernel(
    S, nb, Q, L1, L2,
    f_hbm, a_hbm, v_hbm, h_hbm, out_ref,
    fbuf, abuf, vbuf, hbuf, scale, hinv, part, half, rcore, ry, own, rband,
    f_sem, a_sem, vh_sem, cs_sem, cr_sem, ys_sem, yr_sem, bs_sem, br_sem,
):
    T = a_hbm.shape[0]
    C = out_ref.shape[2]
    zb, X, _ = out_ref.shape
    xs = X // nb
    K = nb // Q
    rows = zb * S * xs
    held = zb * xs
    shots, band = lax.axis_index("shots"), lax.axis_index("band")
    core, y = shots % 2, shots // 2
    other_core = shots + 1 - 2 * core
    other_y = shots + 2 - 4 * y
    first = band // Q

    def group(k):
        return (first + k + 1) % K

    def loads(k):
        at = pl.multiple_of(group(k) * (Q * rows), Q * rows)
        return (
            pltpu.make_async_copy(f_hbm.at[:, pl.ds(at, Q * rows), :], fbuf.at[k], f_sem.at[k]),
            pltpu.make_async_copy(a_hbm.at[:, pl.ds(at, Q * rows), :], abuf.at[k], a_sem.at[k]),
        )

    for k in range(K):
        for c in loads(k):
            c.start()
    mine = pl.ds(pl.multiple_of(shots * C, C), C)
    vcopy = pltpu.make_async_copy(v_hbm.at[:, :, mine], vbuf, vh_sem.at[0])
    hcopy = pltpu.make_async_copy(h_hbm.at[:, :, mine], hbuf, vh_sem.at[1])
    vcopy.start()
    hcopy.start()

    barrier = pltpu.get_barrier_semaphore()
    pl.semaphore_signal(barrier, inc=1, device_id=(other_core, band), device_id_type=MESH)
    pl.semaphore_signal(barrier, inc=1, device_id=(other_y, band), device_id_type=MESH)
    for d in range(1, nb):
        pl.semaphore_signal(barrier, inc=1, device_id=(shots, (band + d) % nb), device_id_type=MESH)
    pl.semaphore_wait(barrier, nb + 1)

    def core_copy(k):
        return pltpu.make_async_remote_copy(
            src_ref=part.at[k, 1 - core], dst_ref=rcore.at[k],
            send_sem=cs_sem.at[k], recv_sem=cr_sem.at[k],
            device_id=(other_core, band), device_id_type=MESH)

    def y_copy(k):
        return pltpu.make_async_remote_copy(
            src_ref=half.at[k, 1 - y], dst_ref=ry.at[k],
            send_sem=ys_sem.at[k], recv_sem=yr_sem.at[k],
            device_id=(other_y, band), device_id_type=MESH)

    def band_copy(k, q, to, source, slot):
        return pltpu.make_async_remote_copy(
            src_ref=own.at[k, q], dst_ref=rband.at[source],
            send_sem=bs_sem.at[slot], recv_sem=br_sem.at[source],
            device_id=(shots, to), device_id_type=MESH)

    def compute(k):
        for c in loads(k):
            c.wait()

        def one(z, _):
            at = pl.multiple_of(z * (S * xs), S * xs)
            here = pl.ds(at, S * xs)
            q, zl = z // zb, z % zb
            f0 = fbuf[k, 0, here, :].astype(jnp.float32)
            f1 = fbuf[k, 1, here, :].astype(jnp.float32)
            d0 = f1 - f0
            acc = None
            for t in range(T):
                f2 = fbuf[k, t + 2, here, :].astype(jnp.float32)
                d1 = f2 - f1
                term = abuf[k, t, here, :].astype(jnp.float32) * (d1 - d0)
                acc = term if acc is None else acc + term
                f1, d0 = f2, d1
            return acc

        for z in range(Q * zb):
            acc = one(z, None)
            for s in range(S):
                part[k, s % 2, s // 2, z * xs:(z + 1) * xs, :] = acc[s * xs:(s + 1) * xs]
        core_copy(k).start()

    def after_core(k):
        core_copy(k).wait_recv()
        half[k] = part[k, core] + rcore[k]
        y_copy(k).start()

    def after_y(k):
        y_copy(k).wait_recv()
        g = group(k)
        for q in range(Q):
            b = g * Q + q
            lo = q * held
            at = pl.multiple_of(b * held, held)
            own[k, q] = (half[k, y, lo:lo + held, :] + ry[k, lo:lo + held, :]) * scale[pl.ds(at, held), :]

            @pl.when(b == band)
            def _():
                rband[band] = own[k, q]

            @pl.when(b != band)
            def _():
                band_copy(k, q, b, band, b).start()

    vcopy.wait()
    for z in range(v_hbm.shape[0]):
        v = vbuf[z]
        scale[z * xs:(z + 1) * xs, :] = 2.0 / (T * (v * v * v))
    hcopy.wait()
    hinv[...] = 1.0 / (hbuf[...] + damping)

    def step(i, _):
        @pl.when(i < K)
        def _():
            compute(i)

        @pl.when((i >= L1) & (i < K + L1))
        def _():
            after_core(i - L1)

        @pl.when(i >= L1 + L2)
        def _():
            after_y(i - L1 - L2)
        return 0

    lax.fori_loop(0, K + L1 + L2, step, 0)

    def put(source, _):
        @pl.when(source != band)
        def _():
            band_copy(0, 0, band, source, source).wait_recv()
        return 0

    lax.fori_loop(0, nb, put, 0)
    for source in range(nb):
        for z in range(zb):
            to = slice(source * xs, (source + 1) * xs)
            out_ref[z, to, :] = rband[source, z * xs:(z + 1) * xs, :] * hinv[z, to, :]

    def drain(k, _):
        core_copy(k).wait_send()
        y_copy(k).wait_send()
        return 0

    lax.fori_loop(0, K, drain, 0)

    def drain_band(b, _):
        @pl.when(b != band)
        def _():
            band_copy(0, 0, b, band, b).wait_send()
        return 0

    lax.fori_loop(0, nb, drain_band, 0)


def shards(S, nb, forward, adjoint, velocity, hessian):
    _, T2, Z, xs, NY = forward.shape
    T = adjoint.shape[1]
    zb, X, _ = hessian.shape
    C = NY // S
    Q = 2
    K = nb // Q
    L1, L2 = 1, 1

    def flat(a):
        a = a[0].reshape(a.shape[1], Z, xs, S, C)
        return a.transpose(0, 1, 3, 2, 4).reshape(a.shape[0], Z * S * xs, C)

    rows, held = zb * S * xs, zb * xs
    bf, f32 = jnp.bfloat16, jnp.float32
    dma = pltpu.SemaphoreType.DMA
    hbm = pl.BlockSpec(memory_space=pltpu.HBM)
    scratch = [
        pltpu.VMEM((K, T2, Q * rows, C), bf),
        pltpu.VMEM((K, T, Q * rows, C), bf),
        pltpu.VMEM((Z, xs, C), f32),
        pltpu.VMEM((zb, X, C), f32),
        pltpu.VMEM((Z * xs, C), f32),
        pltpu.VMEM((zb, X, C), f32),
        pltpu.VMEM((K, 2, 2, Q * held, C), f32),
        pltpu.VMEM((K, 2, Q * held, C), f32),
        pltpu.VMEM((K, 2, Q * held, C), f32),
        pltpu.VMEM((K, Q * held, C), f32),
        pltpu.VMEM((K, Q, held, C), f32),
        pltpu.VMEM((nb, held, C), f32),
        dma((K,)), dma((K,)), dma((2,)),
        dma((K,)), dma((K,)), dma((K,)), dma((K,)), dma((nb,)), dma((nb,)),
    ]
    return pl.pallas_call(
        functools.partial(kernel, S, nb, Q, L1, L2),
        out_shape=jax.ShapeDtypeStruct((zb, X, C), f32),
        in_specs=[hbm] * 4,
        out_specs=pl.BlockSpec(memory_space=pltpu.VMEM),
        scratch_shapes=scratch,
        compiler_params=pltpu.CompilerParams(
            collective_id=0, has_side_effects=True, vmem_limit_bytes=60 * 1024 * 1024
        ),
    )(flat(forward), flat(adjoint), velocity, hessian)


def solution(mesh):
    return jax.shard_map(
        functools.partial(shards, mesh.shape["shots"], mesh.shape["band"]),
        mesh=mesh,
        in_specs=(
            P("shots", None, None, "band", None),
            P("shots", None, None, "band", None),
            P(None, "band", None),
            P("band", None, None),
        ),
        out_specs=P("band", None, "shots"),
        check_vma=False,
    )
```

```python
import functools

import jax
import jax.numpy as jnp
from jax import lax
from jax.experimental import pallas as pl
from jax.experimental.pallas import tpu as pltpu
from jax.sharding import PartitionSpec as P

damping = 0.05
MESH = pl.DeviceIdType.MESH


def kernel(
    S, nb, Q,
    f_hbm, a_hbm, v_hbm, h_hbm, out_ref,
    fbuf, abuf, vbuf, hbuf, scale, hinv, part, half, rcore, rband,
    f_sem, a_sem, vh_sem, cs_sem, cr_sem, bs_sem, br_sem,
):
    T = a_hbm.shape[0]
    C = out_ref.shape[2]
    zb, X, _ = out_ref.shape
    xs = X // nb
    K = nb // Q
    rows = zb * S * xs
    held = zb * xs
    shots, band = lax.axis_index("shots"), lax.axis_index("band")
    core, y = shots % 2, shots // 2
    other_core = shots + 1 - 2 * core
    other_y = shots + 2 - 4 * y
    first = band // Q

    def group(k):
        return (first + k + 1) % K

    def loads(k):
        at = pl.multiple_of(group(k) * (Q * rows), Q * rows)
        return (
            pltpu.make_async_copy(f_hbm.at[:, pl.ds(at, Q * rows), :], fbuf.at[k], f_sem.at[k]),
            pltpu.make_async_copy(a_hbm.at[:, pl.ds(at, Q * rows), :], abuf.at[k], a_sem.at[k]),
        )

    for k in range(K):
        for c in loads(k):
            c.start()
    mine = pl.ds(pl.multiple_of(shots * C, C), C)
    vcopies = [
        pltpu.make_async_copy(
            v_hbm.at[:, :, pl.ds(pl.multiple_of((core + 2 * i) * C, C), C)], vbuf.at[i], vh_sem.at[i + 1])
        for i in range(2)
    ]
    hcopy = pltpu.make_async_copy(h_hbm.at[:, :, mine], hbuf, vh_sem.at[0])
    for c in vcopies:
        c.start()
    hcopy.start()

    barrier = pltpu.get_barrier_semaphore()
    pl.semaphore_signal(barrier, inc=1, device_id=(other_core, band), device_id_type=MESH)
    pl.semaphore_signal(barrier, inc=1, device_id=(other_y, band), device_id_type=MESH)
    for d in range(1, nb):
        pl.semaphore_signal(barrier, inc=1, device_id=(shots, (band + d) % nb), device_id_type=MESH)
        pl.semaphore_signal(barrier, inc=1, device_id=(other_y, (band + d) % nb), device_id_type=MESH)

    def core_copy(k):
        return pltpu.make_async_remote_copy(
            src_ref=part.at[k, 1 - core], dst_ref=rcore.at[k],
            send_sem=cs_sem.at[k], recv_sem=cr_sem.at[k],
            device_id=(other_core, band), device_id_type=MESH)

    def band_copy(k, q, toy, to, sy, source):
        return pltpu.make_async_remote_copy(
            src_ref=half.at[k, toy, q], dst_ref=rband.at[sy, source],
            send_sem=bs_sem.at[toy, to], recv_sem=br_sem.at[sy, source],
            device_id=(core + 2 * toy, to), device_id_type=MESH)

    def compute(k):
        for c in loads(k):
            c.wait()

        def one(z, _):
            at = pl.multiple_of(z * (S * xs), S * xs)
            here = pl.ds(at, S * xs)
            q, zl = z // zb, z % zb
            f0 = fbuf[k, 0, here, :].astype(jnp.float32)
            f1 = fbuf[k, 1, here, :].astype(jnp.float32)
            d0 = f1 - f0
            acc = None
            for t in range(T):
                f2 = fbuf[k, t + 2, here, :].astype(jnp.float32)
                d1 = f2 - f1
                term = abuf[k, t, here, :].astype(jnp.float32) * (d1 - d0)
                acc = term if acc is None else acc + term
                f1, d0 = f2, d1
            return acc

        for z in range(Q * zb):
            acc = one(z, None)
            for s in range(S):
                part[k, s % 2, s // 2, z * xs:(z + 1) * xs, :] = acc[s * xs:(s + 1) * xs]

    def after_core(k):
        core_copy(k).wait_recv()
        g = group(k)
        for q in range(Q):
            b = g * Q + q
            lo = q * held
            at = pl.multiple_of(b * held, held)
            for toy in range(2):
                half[k, toy, q] = (
                    part[k, core, toy, lo:lo + held, :] + rcore[k, toy, lo:lo + held, :]
                ) * scale[toy, pl.ds(at, held), :]
        for q in range(Q):
            b = g * Q + q
            for toy in range(2):
                @pl.when((b == band) & (toy == y))
                def _():
                    rband[y, band] = half[k, toy, q]

                @pl.when((b != band) | (toy != y))
                def _():
                    band_copy(k, q, toy, b, y, band).start()

    for i in range(2):
        vcopies[i].wait()
        for z in range(v_hbm.shape[0]):
            v = vbuf[i, z]
            scale[i, z * xs:(z + 1) * xs, :] = 2.0 / (T * (v * v * v))
    hcopy.wait()
    hinv[...] = 1.0 / (hbuf[...] + damping)

    def work(k, _):
        compute(k)
        return 0

    lax.fori_loop(0, K, work, 0)
    pl.semaphore_wait(barrier, 2 * nb)

    def send(k, _):
        core_copy(k).start()
        return 0

    lax.fori_loop(0, K, send, 0)

    def step(k, _):
        after_core(k)
        return 0

    lax.fori_loop(0, K, step, 0)

    def put(source, _):
        for sy in range(2):
            @pl.when((source != band) | (sy != y))
            def _():
                band_copy(0, 0, sy, source, sy, source).wait_recv()
        return 0

    lax.fori_loop(0, nb, put, 0)
    for source in range(nb):
        for z in range(zb):
            to = slice(source * xs, (source + 1) * xs)
            rows_z = slice(z * xs, (z + 1) * xs)
            out_ref[z, to, :] = (rband[0, source, rows_z, :] + rband[1, source, rows_z, :]) * hinv[z, to, :]

    def drain(k, _):
        core_copy(k).wait_send()
        return 0

    lax.fori_loop(0, K, drain, 0)

    def drain_band(b, _):
        for toy in range(2):
            @pl.when((b != band) | (toy != y))
            def _():
                band_copy(0, 0, toy, b, y, band).wait_send()
        return 0

    lax.fori_loop(0, nb, drain_band, 0)


def shards(S, nb, forward, adjoint, velocity, hessian):
    _, T2, Z, xs, NY = forward.shape
    T = adjoint.shape[1]
    zb, X, _ = hessian.shape
    C = NY // S
    Q = 4
    K = nb // Q

    def flat(a):
        a = a[0].reshape(a.shape[1], Z, xs, S, C)
        return a.transpose(0, 1, 3, 2, 4).reshape(a.shape[0], Z * S * xs, C)

    rows, held = zb * S * xs, zb * xs
    bf, f32 = jnp.bfloat16, jnp.float32
    dma = pltpu.SemaphoreType.DMA
    hbm = pl.BlockSpec(memory_space=pltpu.HBM)
    scratch = [
        pltpu.VMEM((K, T2, Q * rows, C), bf),
        pltpu.VMEM((K, T, Q * rows, C), bf),
        pltpu.VMEM((2, Z, xs, C), f32),
        pltpu.VMEM((zb, X, C), f32),
        pltpu.VMEM((2, Z * xs, C), f32),
        pltpu.VMEM((zb, X, C), f32),
        pltpu.VMEM((K, 2, 2, Q * held, C), f32),
        pltpu.VMEM((K, 2, Q, held, C), f32),
        pltpu.VMEM((K, 2, Q * held, C), f32),
        pltpu.VMEM((2, nb, held, C), f32),
        dma((K,)), dma((K,)), dma((3,)),
        dma((K,)), dma((K,)), dma((2, nb)), dma((2, nb)),
    ]
    return pl.pallas_call(
        functools.partial(kernel, S, nb, Q),
        out_shape=jax.ShapeDtypeStruct((zb, X, C), f32),
        in_specs=[hbm] * 4,
        out_specs=pl.BlockSpec(memory_space=pltpu.VMEM),
        scratch_shapes=scratch,
        compiler_params=pltpu.CompilerParams(
            collective_id=0, has_side_effects=True, vmem_limit_bytes=60 * 1024 * 1024
        ),
    )(flat(forward), flat(adjoint), velocity, hessian)


def solution(mesh):
    return jax.shard_map(
        functools.partial(shards, mesh.shape["shots"], mesh.shape["band"]),
        mesh=mesh,
        in_specs=(
            P("shots", None, None, "band", None),
            P("shots", None, None, "band", None),
            P(None, "band", None),
            P("band", None, None),
        ),
        out_specs=P("band", None, "shots"),
        check_vma=False,
    )
```

```python
import functools

import jax
import jax.numpy as jnp
from jax import lax
from jax.experimental import pallas as pl
from jax.experimental.pallas import tpu as pltpu
from jax.sharding import PartitionSpec as P

damping = 0.05
MESH = pl.DeviceIdType.MESH


def kernel(
    S, nb, Q,
    f_hbm, a_hbm, v_hbm, h_hbm, out_ref,
    fbuf, abuf, vbuf, hbuf, scale, hinv, part, half, rcore, rband,
    f_sem, a_sem, vh_sem, cs_sem, cr_sem, bs_sem, br_sem,
):
    T = a_hbm.shape[0]
    C = out_ref.shape[2]
    zb, X, _ = out_ref.shape
    xs = X // nb
    K = nb // Q
    rows = zb * S * xs
    held = zb * xs
    shots, band = lax.axis_index("shots"), lax.axis_index("band")
    core, y = shots % 2, shots // 2
    other_core = shots + 1 - 2 * core
    other_y = shots + 2 - 4 * y
    first = band // Q

    def group(k):
        return (first + k + 1) % K

    def loads(k):
        at = pl.multiple_of(group(k) * (Q * rows), Q * rows)
        return (
            pltpu.make_async_copy(f_hbm.at[:, pl.ds(at, Q * rows), :], fbuf.at[k], f_sem.at[k]),
            pltpu.make_async_copy(a_hbm.at[:, pl.ds(at, Q * rows), :], abuf.at[k], a_sem.at[k]),
        )

    for c in loads(0):
        c.start()
    mine = pl.ds(pl.multiple_of(shots * C, C), C)
    vcopies = [
        pltpu.make_async_copy(
            v_hbm.at[:, :, pl.ds(pl.multiple_of((core + 2 * i) * C, C), C)], vbuf.at[i], vh_sem.at[i + 1])
        for i in range(2)
    ]
    hcopy = pltpu.make_async_copy(h_hbm.at[:, :, mine], hbuf, vh_sem.at[0])
    for c in vcopies:
        c.start()
    for k in range(1, K):
        for c in loads(k):
            c.start()
    hcopy.start()

    barrier = pltpu.get_barrier_semaphore()
    pl.semaphore_signal(barrier, inc=1, device_id=(other_core, band), device_id_type=MESH)
    pl.semaphore_signal(barrier, inc=1, device_id=(other_y, band), device_id_type=MESH)
    for d in range(1, nb):
        pl.semaphore_signal(barrier, inc=1, device_id=(shots, (band + d) % nb), device_id_type=MESH)
        pl.semaphore_signal(barrier, inc=1, device_id=(other_y, (band + d) % nb), device_id_type=MESH)

    def core_copy(k):
        return pltpu.make_async_remote_copy(
            src_ref=part.at[k, 1 - core], dst_ref=rcore.at[k],
            send_sem=cs_sem.at[k], recv_sem=cr_sem.at[k],
            device_id=(other_core, band), device_id_type=MESH)

    def band_copy(k, q, toy, to, sy, source):
        return pltpu.make_async_remote_copy(
            src_ref=half.at[k, toy, q], dst_ref=rband.at[sy, source],
            send_sem=bs_sem.at[toy, to], recv_sem=br_sem.at[sy, source],
            device_id=(core + 2 * toy, to), device_id_type=MESH)

    def compute(k):
        for c in loads(k):
            c.wait()

        def one(z, _):
            at = pl.multiple_of(z * (S * xs), S * xs)
            here = pl.ds(at, S * xs)
            q, zl = z // zb, z % zb
            f0 = fbuf[k, 0, here, :].astype(jnp.float32)
            f1 = fbuf[k, 1, here, :].astype(jnp.float32)
            d0 = f1 - f0
            acc = None
            for t in range(T):
                f2 = fbuf[k, t + 2, here, :].astype(jnp.float32)
                d1 = f2 - f1
                term = abuf[k, t, here, :].astype(jnp.float32) * (d1 - d0)
                acc = term if acc is None else acc + term
                f1, d0 = f2, d1
            return acc

        for z in range(Q * zb):
            acc = one(z, None)
            for s in range(S):
                part[k, s % 2, s // 2, z * xs:(z + 1) * xs, :] = acc[s * xs:(s + 1) * xs]

    def after_core(k):
        core_copy(k).wait_recv()
        g = group(k)
        for q in range(Q):
            b = g * Q + q
            lo = q * held
            at = pl.multiple_of(b * held, held)
            for toy in range(2):
                half[k, toy, q] = (
                    part[k, core, toy, lo:lo + held, :] + rcore[k, toy, lo:lo + held, :]
                ) * scale[toy, pl.ds(at, held), :]
        for q in range(Q):
            b = g * Q + q
            for toy in range(2):
                @pl.when((b == band) & (toy == y))
                def _():
                    rband[y, band] = half[k, toy, q]

                @pl.when((b != band) | (toy != y))
                def _():
                    band_copy(k, q, toy, b, y, band).start()

    for k in range(1):
        compute(k)
    pl.semaphore_wait(barrier, 2 * nb)
    for k in range(1):
        core_copy(k).start()

    for i in range(2):
        vcopies[i].wait()
        for z in range(v_hbm.shape[0]):
            v = vbuf[i, z]
            scale[i, z * xs:(z + 1) * xs, :] = 2.0 / (T * (v * v * v))

    def step(k, _):
        compute(k)
        core_copy(k).start()
        after_core(k - 1)
        return 0

    lax.fori_loop(1, K, step, 0)

    def tail(k, _):
        after_core(k)
        return 0

    lax.fori_loop(K - 1, K, tail, 0)

    hcopy.wait()
    hinv[...] = 1.0 / (hbuf[...] + damping)

    def put(source, _):
        for sy in range(2):
            @pl.when((source != band) | (sy != y))
            def _():
                band_copy(0, 0, sy, source, sy, source).wait_recv()
        return 0

    lax.fori_loop(0, nb, put, 0)
    for source in range(nb):
        for z in range(zb):
            to = slice(source * xs, (source + 1) * xs)
            rows_z = slice(z * xs, (z + 1) * xs)
            out_ref[z, to, :] = (rband[0, source, rows_z, :] + rband[1, source, rows_z, :]) * hinv[z, to, :]

    def drain(k, _):
        core_copy(k).wait_send()
        return 0

    lax.fori_loop(0, K, drain, 0)

    def drain_band(b, _):
        for toy in range(2):
            @pl.when((b != band) | (toy != y))
            def _():
                band_copy(0, 0, toy, b, y, band).wait_send()
        return 0

    lax.fori_loop(0, nb, drain_band, 0)


def shards(S, nb, forward, adjoint, velocity, hessian):
    _, T2, Z, xs, NY = forward.shape
    T = adjoint.shape[1]
    zb, X, _ = hessian.shape
    C = NY // S
    Q = 4
    K = nb // Q

    def flat(a):
        a = a[0].reshape(a.shape[1], Z, xs, S, C)
        return a.transpose(0, 1, 3, 2, 4).reshape(a.shape[0], Z * S * xs, C)

    rows, held = zb * S * xs, zb * xs
    bf, f32 = jnp.bfloat16, jnp.float32
    dma = pltpu.SemaphoreType.DMA
    hbm = pl.BlockSpec(memory_space=pltpu.HBM)
    scratch = [
        pltpu.VMEM((K, T2, Q * rows, C), bf),
        pltpu.VMEM((K, T, Q * rows, C), bf),
        pltpu.VMEM((2, Z, xs, C), f32),
        pltpu.VMEM((zb, X, C), f32),
        pltpu.VMEM((2, Z * xs, C), f32),
        pltpu.VMEM((zb, X, C), f32),
        pltpu.VMEM((K, 2, 2, Q * held, C), f32),
        pltpu.VMEM((K, 2, Q, held, C), f32),
        pltpu.VMEM((K, 2, Q * held, C), f32),
        pltpu.VMEM((2, nb, held, C), f32),
        dma((K,)), dma((K,)), dma((3,)),
        dma((K,)), dma((K,)), dma((2, nb)), dma((2, nb)),
    ]
    return pl.pallas_call(
        functools.partial(kernel, S, nb, Q),
        out_shape=jax.ShapeDtypeStruct((zb, X, C), f32),
        in_specs=[hbm] * 4,
        out_specs=pl.BlockSpec(memory_space=pltpu.VMEM),
        scratch_shapes=scratch,
        compiler_params=pltpu.CompilerParams(
            collective_id=0, has_side_effects=True, vmem_limit_bytes=60 * 1024 * 1024
        ),
    )(flat(forward), flat(adjoint), velocity, hessian)


def solution(mesh):
    return jax.shard_map(
        functools.partial(shards, mesh.shape["shots"], mesh.shape["band"]),
        mesh=mesh,
        in_specs=(
            P("shots", None, None, "band", None),
            P("shots", None, None, "band", None),
            P(None, "band", None),
            P("band", None, None),
        ),
        out_specs=P("band", None, "shots"),
        check_vma=False,
    )
```

```python
import functools

import jax
import jax.numpy as jnp
from jax import lax
from jax.experimental import pallas as pl
from jax.experimental.pallas import tpu as pltpu
from jax.sharding import PartitionSpec as P

damping = 0.05
MESH = pl.DeviceIdType.MESH


def kernel(
    S, nb, Q,
    f_hbm, a_hbm, v_hbm, h_hbm, out_ref,
    fbuf, abuf, vbuf, hbuf, scale, hinv, part, half, rcore, rband,
    f_sem, a_sem, vh_sem, cs_sem, cr_sem, bs_sem, br_sem,
):
    T = a_hbm.shape[0]
    C = out_ref.shape[2]
    zb, X, _ = out_ref.shape
    xs = X // nb
    K = nb // Q
    rows = zb * S * xs
    held = zb * xs
    shots, band = lax.axis_index("shots"), lax.axis_index("band")
    core, y = shots % 2, shots // 2
    other_core = shots + 1 - 2 * core
    other_y = shots + 2 - 4 * y
    first = band // Q

    def group(k):
        return (first + k + 1) % K

    def loads(k):
        at = pl.multiple_of(group(k) * (Q * rows), Q * rows)
        return (
            pltpu.make_async_copy(f_hbm.at[:, pl.ds(at, Q * rows), :], fbuf.at[k], f_sem.at[k]),
            pltpu.make_async_copy(a_hbm.at[:, pl.ds(at, Q * rows), :], abuf.at[k], a_sem.at[k]),
        )

    for c in loads(0):
        c.start()
    mine = pl.ds(pl.multiple_of(shots * C, C), C)
    vcopies = [
        pltpu.make_async_copy(
            v_hbm.at[:, :, pl.ds(pl.multiple_of((core + 2 * i) * C, C), C)], vbuf.at[i], vh_sem.at[i + 1])
        for i in range(2)
    ]
    hcopy = pltpu.make_async_copy(h_hbm.at[:, :, mine], hbuf, vh_sem.at[0])
    for c in vcopies:
        c.start()
    for k in range(1, K):
        for c in loads(k):
            c.start()
    hcopy.start()

    barrier = pltpu.get_barrier_semaphore()
    pl.semaphore_signal(barrier, inc=1, device_id=(other_core, band), device_id_type=MESH)
    pl.semaphore_signal(barrier, inc=1, device_id=(other_y, band), device_id_type=MESH)
    for d in range(1, nb):
        pl.semaphore_signal(barrier, inc=1, device_id=(shots, (band + d) % nb), device_id_type=MESH)
        pl.semaphore_signal(barrier, inc=1, device_id=(other_y, (band + d) % nb), device_id_type=MESH)

    def core_copy(k):
        return pltpu.make_async_remote_copy(
            src_ref=part.at[k, 1 - core], dst_ref=rcore.at[k],
            send_sem=cs_sem.at[k], recv_sem=cr_sem.at[k],
            device_id=(other_core, band), device_id_type=MESH)

    def band_copy(k, q, toy, to, sy, source):
        return pltpu.make_async_remote_copy(
            src_ref=half.at[k, toy, q], dst_ref=rband.at[sy, source],
            send_sem=bs_sem.at[toy, to], recv_sem=br_sem.at[sy, source],
            device_id=(core + 2 * toy, to), device_id_type=MESH)

    def compute(k):
        for c in loads(k):
            c.wait()

        def one(z, _):
            at = pl.multiple_of(z * (S * xs), S * xs)
            here = pl.ds(at, S * xs)
            q, zl = z // zb, z % zb
            f0 = fbuf[k, 0, here, :].astype(jnp.float32)
            f1 = fbuf[k, 1, here, :].astype(jnp.float32)
            d0 = f1 - f0
            acc = None
            for t in range(T):
                f2 = fbuf[k, t + 2, here, :].astype(jnp.float32)
                d1 = f2 - f1
                term = abuf[k, t, here, :].astype(jnp.float32) * (d1 - d0)
                acc = term if acc is None else acc + term
                f1, d0 = f2, d1
            return acc

        for z in range(Q * zb):
            acc = one(z, None)
            for s in range(S):
                part[k, s % 2, s // 2, z * xs:(z + 1) * xs, :] = acc[s * xs:(s + 1) * xs]

    def after_core(k):
        core_copy(k).wait_recv()
        g = group(k)
        for q in range(Q):
            b = g * Q + q
            lo = q * held
            at = pl.multiple_of(b * held, held)
            for toy in range(2):
                half[k, toy, q] = (
                    part[k, core, toy, lo:lo + held, :] + rcore[k, toy, lo:lo + held, :]
                ) * scale[toy, pl.ds(at, held), :]
        for q in range(Q):
            b = g * Q + q
            for toy in range(2):
                @pl.when((b == band) & (toy == y))
                def _():
                    rband[y, band] = half[k, toy, q]

                @pl.when((b != band) | (toy != y))
                def _():
                    band_copy(k, q, toy, b, y, band).start()

    for k in range(1):
        compute(k)
    pl.semaphore_wait(barrier, 2 * nb)
    for k in range(1):
        core_copy(k).start()

    for i in range(2):
        vcopies[i].wait()
        for z in range(v_hbm.shape[0]):
            v = vbuf[i, z]
            scale[i, z * xs:(z + 1) * xs, :] = 2.0 / (T * (v * v * v))

    def step(k, _):
        compute(k)
        core_copy(k).start()
        after_core(k - 1)
        return 0

    lax.fori_loop(1, K, step, 0)

    def tail(k, _):
        after_core(k)
        return 0

    lax.fori_loop(K - 1, K, tail, 0)

    hcopy.wait()
    hinv[...] = 1.0 / (hbuf[...] + damping)

    def put(source, _):
        for sy in range(2):
            @pl.when((source != band) | (sy != y))
            def _():
                band_copy(0, 0, sy, source, sy, source).wait_recv()
        return 0

    lax.fori_loop(0, nb, put, 0)
    for source in range(nb):
        for z in range(zb):
            to = slice(source * xs, (source + 1) * xs)
            rows_z = slice(z * xs, (z + 1) * xs)
            out_ref[z, to, :] = (rband[0, source, rows_z, :] + rband[1, source, rows_z, :]) * hinv[z, to, :]

    def drain(k, _):
        core_copy(k).wait_send()
        return 0

    lax.fori_loop(0, K, drain, 0)

    def drain_band(b, _):
        for toy in range(2):
            @pl.when((b != band) | (toy != y))
            def _():
                band_copy(0, 0, toy, b, y, band).wait_send()
        return 0

    lax.fori_loop(0, nb, drain_band, 0)


def shards(S, nb, forward, adjoint, velocity, hessian):
    _, T2, Z, xs, NY = forward.shape
    T = adjoint.shape[1]
    zb, X, _ = hessian.shape
    C = NY // S
    Q = 4
    K = nb // Q

    def flat(a):
        a = a[0].reshape(a.shape[1], Z, xs, S, C)
        return a.transpose(0, 1, 3, 2, 4).reshape(a.shape[0], Z * S * xs, C)

    rows, held = zb * S * xs, zb * xs
    bf, f32 = jnp.bfloat16, jnp.float32
    dma = pltpu.SemaphoreType.DMA
    hbm = pl.BlockSpec(memory_space=pltpu.HBM)
    scratch = [
        pltpu.VMEM((K, T2, Q * rows, C), bf),
        pltpu.VMEM((K, T, Q * rows, C), bf),
        pltpu.VMEM((2, Z, xs, C), f32),
        pltpu.VMEM((zb, X, C), f32),
        pltpu.VMEM((2, Z * xs, C), f32),
        pltpu.VMEM((zb, X, C), f32),
        pltpu.VMEM((K, 2, 2, Q * held, C), f32),
        pltpu.VMEM((K, 2, Q, held, C), f32),
        pltpu.VMEM((K, 2, Q * held, C), f32),
        pltpu.VMEM((2, nb, held, C), f32),
        dma((K,)), dma((K,)), dma((3,)),
        dma((K,)), dma((K,)), dma((2, nb)), dma((2, nb)),
    ]
    return pl.pallas_call(
        functools.partial(kernel, S, nb, Q),
        out_shape=jax.ShapeDtypeStruct((zb, X, C), f32),
        in_specs=[hbm] * 4,
        out_specs=pl.BlockSpec(memory_space=pltpu.VMEM),
        scratch_shapes=scratch,
        compiler_params=pltpu.CompilerParams(
            collective_id=0, has_side_effects=True, vmem_limit_bytes=56360960
        ),
    )(flat(forward), flat(adjoint), velocity, hessian)


def solution(mesh):
    return jax.shard_map(
        functools.partial(shards, mesh.shape["shots"], mesh.shape["band"]),
        mesh=mesh,
        in_specs=(
            P("shots", None, None, "band", None),
            P("shots", None, None, "band", None),
            P(None, "band", None),
            P("band", None, None),
        ),
        out_specs=P("band", None, "shots"),
        check_vma=False,
    )
```
